256 devices in a mesh: row: 16 (over x, z_hi, core), col: 4 (over z_lo), depth: 4 (over y).
Axes of the slice: x: 4, y: 4, z: 8 (z_hi: 2, z_lo: 4; z = z_hi * 4 + z_lo), core: 2. Of those that a mesh axis runs over, the one named last changes fastest.
Arguments:
- density: float32 [1024, 5, 128, 128], P('row', None, ('col', 'depth')), may hold values from -1 to 1
- mask_band: int32 [1024, 5], P('row'), may hold values 0 or 1
- mask_square: int32 [1024, 9], P('row'), may hold values 0 or 1
- mask_out: int32 [1024, 5], P('row'), may hold values 0 or 1
Outputs:
- purified: float32 [1024, 5, 128, 128], P('row', None, ('col', 'depth'))
The draws below stay inside these ranges and needn't reach their ends.
All inputs are finite; a program needn't handle non-finite values. No bound on the sum of `mask_band` or of `mask_square` or of `mask_out` on one device may be relied on, other than what follows from the above.
Results may differ from the reference program's by a relative error of at most 0.0003.
Values sent between devices are 32-bit elements; how exact they have to be, the bound alone decides.
No kernel may reach another device: no remote copies, remote signals or barrier semaphores. Data moves between devices by JAX's collectives and lax.ppermute only.
A program may use at most 64 MiB of HBM per device.

```python
import jax
import jax.numpy as jnp
from jax import lax

BLK = 128
BROWS = 4
NB = 1024


def touch_ends(array, stream_key, least, largest):
    index_at = [jax.random.randint(jax.random.fold_in(stream_key, axis), (), 0, length) for axis, length in enumerate(array.shape)]
    main_axis = array.shape.index(max(array.shape))
    beside = index_at[:main_axis] + [(index_at[main_axis] + 1) % array.shape[main_axis]] + index_at[main_axis + 1:]
    return array.at[tuple(index_at)].set(least).at[tuple(beside)].set(largest)


def block_levels(rng, dims, pieces, low, top_value):
    def one(axis_at, blocks):
        steps = jax.random.uniform(jax.random.fold_in(jax.random.fold_in(rng, 6), axis_at), (blocks,), jnp.float32, low / len(pieces), top_value / len(pieces))
        return jnp.repeat(jnp.exp(steps), dims[axis_at] // blocks).reshape((-1,) + (1,) * (len(dims) - axis_at - 1))

    level = one(*pieces[0])
    for cut in pieces[1:]:
        level = level * one(*cut)
    return level


def centred(stream_key, shape, spread, most, pieces=(), held_as=jnp.bfloat16):
    values = spread * jax.random.normal(stream_key, shape, jnp.float32)
    if pieces:
        values = values * block_levels(stream_key, shape, pieces, -0.22, 0.18)
    return jnp.clip(values, -most, most).astype(held_as)


def setup_inputs(seed: int = 0) -> dict:
    seeds = jax.random.split(jax.random.key(seed), 5)
    return {
        "density": centred(seeds[0], (NB, 5, BLK, BLK), (BLK // 3) ** -0.5, 1.0, ((0, 16), (2, 16)), jnp.float32),
        "mask_band": touch_ends((jax.random.randint(seeds[1], (NB, 5), 0, 4) < 3).astype(jnp.int32), jax.random.fold_in(seeds[1], 1), 0, 1),
        "mask_square": touch_ends((jax.random.randint(seeds[2], (NB, 9), 0, 4) < 3).astype(jnp.int32), jax.random.fold_in(seeds[2], 1), 0, 1),
        "mask_out": touch_ends((jax.random.randint(seeds[3], (NB, 5), 0, 4) < 3).astype(jnp.int32), jax.random.fold_in(seeds[3], 1), 0, 1),
    }


def square_band(left_band, widened, margin):
    span_rows = left_band.shape[0]
    square = jnp.zeros((span_rows, 9, left_band.shape[2], left_band.shape[3]), jnp.float32)
    for offset in range(5):
        lower = offset - 2 + margin
        product = jnp.einsum("rab,rubc->ruac", left_band[:, offset], widened[lower:lower + span_rows], precision=lax.Precision.HIGHEST)
        square = square.at[:, offset:offset + 5].add(product)
    return square


def cube_left(square, widened):
    span_rows = square.shape[0]
    result = jnp.zeros((span_rows, 5, square.shape[2], square.shape[3]), jnp.float32)
    for column in range(9):
        lowest = max(0, 4 - column)
        highest = min(4, 8 - column)
        product = jnp.einsum("rab,rubc->ruac", square[:, column], widened[column:column + span_rows, lowest:highest + 1], precision=lax.Precision.HIGHEST)
        result = result.at[:, lowest + column - 4:highest + column - 3].add(product)
    return result


def reference(density, mask_band, mask_square, mask_out):
    columns = jnp.arange(NB, dtype=jnp.int32)[:, None] + jnp.arange(5, dtype=jnp.int32)[None, :] - 2
    inside = ((columns >= 0) & (columns < NB)).astype(jnp.float32)
    weight = mask_band.astype(jnp.float32) * inside
    active = density * weight[:, :, None, None]
    padded = jnp.pad(active, ((4, 4), (0, 0), (0, 0), (0, 0)))
    square_gate = mask_square.astype(jnp.float32).reshape(NB // BROWS, BROWS, 9)
    output_gate = mask_out.astype(jnp.float32).reshape(NB // BROWS, BROWS, 5)

    def one_group(inputs):
        group_index, square_mask, output_mask = inputs
        first_row = (group_index * BROWS).astype(jnp.int32)
        widened = lax.dynamic_slice_in_dim(padded, first_row, BROWS + 8, 0)
        owned_rows = widened[4:4 + BROWS]
        square = square_band(owned_rows, widened, 4) * square_mask[:, :, None, None]
        cube_part = cube_left(square, widened)
        return output_mask[:, :, None, None] * (3.0 * square[:, 2:7] - 2.0 * cube_part)

    blocks = lax.map(one_group, (jnp.arange(NB // BROWS, dtype=jnp.int32), square_gate, output_gate))
    return blocks.reshape(density.shape)
```

```python
import jax
import jax.numpy as jnp
from jax import lax
from jax.experimental import pallas as pl
from jax.experimental.pallas import tpu as pltpu
from jax.sharding import PartitionSpec as P

BLK = 128
OWN = 4
HALO = 4
PAIR = 2 * BLK
LAYERS = ("col", "depth")
EVERY = ("row", "col", "depth")

TO_BEFORE = [(0, s) for s in range(5)] + [(1, s) for s in range(5)] + [(2, 0), (2, 1), (3, 0)]
TO_AFTER = [(0, 4), (1, 3), (1, 4)] + [(2, s) for s in range(5)] + [(3, s) for s in range(5)]


def put_block(row, slot, value, high, low):
    top = row * BLK
    left = (row + slot - 2) * BLK
    rounded = value.astype(jnp.bfloat16)
    high[top : top + BLK, left : left + BLK] = rounded
    low[top : top + BLK, left : left + BLK] = (value - rounded.astype(jnp.float32)).astype(jnp.bfloat16)


def product(left_high, left_low, right_high, right_low):
    def dot(a, b):
        return jnp.dot(a, b, preferred_element_type=jnp.float32)

    return dot(left_high, right_high) + (dot(left_high, right_low) + dot(left_low, right_high))


def compute_kernel(own, after, before, square_mask, out_mask, out, high, low, square_high, square_low):
    first = lax.axis_index(LAYERS) * OWN
    zero = jnp.zeros((BLK, BLK), jnp.bfloat16)
    for pair in range(1, 5):
        for row, column in ((2 * pair + 1, 2 * pair - 2), (2 * pair, 2 * pair + 3)):
            high[row * BLK : (row + 1) * BLK, column * BLK : (column + 1) * BLK] = zero
            low[row * BLK : (row + 1) * BLK, column * BLK : (column + 1) * BLK] = zero
    for row, column in ((0, 3), (11, 8)):
        high[row * BLK : (row + 1) * BLK, column * BLK : (column + 1) * BLK] = zero
        low[row * BLK : (row + 1) * BLK, column * BLK : (column + 1) * BLK] = zero
    for place, (row, slot) in enumerate(TO_AFTER):
        put_block(row, slot, before[:, place].reshape(BLK, BLK), high, low)
    for row in range(OWN):
        for slot in range(5):
            put_block(HALO + row, slot, own[:, row * 5 + slot].reshape(BLK, BLK), high, low)
    for place, (row, slot) in enumerate(TO_BEFORE):
        put_block(HALO + OWN + row, slot, after[:, place].reshape(BLK, BLK), high, low)

    def tile(low_index, high_index):
        return slice(low_index * PAIR, high_index * PAIR)

    for pair in (2, 3):
        mine = tile(pair, pair + 1)
        kept = {}
        for column in range(pair - 2, pair + 3):
            inner = tile(max(pair, column) - 1, min(pair, column) + 2)
            outer = tile(column, column + 1)
            square = product(high[mine, inner], low[mine, inner], high[inner, outer], low[inner, outer])
            for half in range(2):
                for side in range(2):
                    slot = 2 * (column - pair) + side - half + 4
                    block = square[half * BLK : (half + 1) * BLK, side * BLK : (side + 1) * BLK]
                    row = 2 * (pair - 2) + half
                    if 0 <= slot < 9:
                        block = block * square_mask[first + row, slot].astype(jnp.float32)
                    if 2 <= slot < 7:
                        kept[row, slot - 2] = block
                    rounded = block.astype(jnp.bfloat16)
                    rows = slice(half * BLK, (half + 1) * BLK)
                    columns = slice(column * PAIR + side * BLK, column * PAIR + (side + 1) * BLK)
                    square_high[rows, columns] = rounded
                    square_low[rows, columns] = (block - rounded.astype(jnp.float32)).astype(jnp.bfloat16)
        for column in range(pair - 1, pair + 2):
            inner = tile(column - 1, column + 2)
            outer = tile(column, column + 1)
            cube = product(square_high[:, inner], square_low[:, inner], high[inner, outer], low[inner, outer])
            for half in range(2):
                for side in range(2):
                    slot = 2 * (column - pair) + side - half + 2
                    row = 2 * (pair - 2) + half
                    if 0 <= slot < 5:
                        block = cube[half * BLK : (half + 1) * BLK, side * BLK : (side + 1) * BLK]
                        gate = out_mask[first + row, slot].astype(jnp.float32)
                        block = gate * (3.0 * kept[row, slot] - 2.0 * block)
                        out[:, row * 5 + slot] = block.reshape(16, 8, BLK)


def compute(own, after, before, square_mask, out_mask):
    vmem = pl.BlockSpec(memory_space=pltpu.VMEM)
    smem = pl.BlockSpec(memory_space=pltpu.SMEM)
    window = (OWN + 2 * HALO) * BLK
    return pl.pallas_call(
        compute_kernel,
        out_shape=jax.ShapeDtypeStruct((16, 5 * OWN, 8, BLK), jnp.float32),
        in_specs=[vmem, vmem, vmem, smem, smem],
        out_specs=vmem,
        scratch_shapes=[
            pltpu.VMEM((window, window), jnp.bfloat16),
            pltpu.VMEM((window, window), jnp.bfloat16),
            pltpu.VMEM((PAIR, window), jnp.bfloat16),
            pltpu.VMEM((PAIR, window), jnp.bfloat16),
        ],
        compiler_params=pltpu.CompilerParams(vmem_limit_bytes=48 * 1024 * 1024),
        cost_estimate=pl.CostEstimate(flops=2 * 3 * 36 * 256**3, bytes_accessed=6 * 1024 * 1024, transcendentals=0),
    )(own, after, before, square_mask, out_mask)


def active_band(density, mask_band, first_row, total_rows):
    columns = (
        first_row
        + jnp.arange(density.shape[0], dtype=jnp.int32)[:, None]
        + jnp.arange(5, dtype=jnp.int32)[None, :]
        - 2
    )
    inside = ((columns >= 0) & (columns < total_rows)).astype(jnp.float32)
    return density * (mask_band.astype(jnp.float32) * inside)[:, :, None, None]


def on_device(density, mask_band, mask_square, mask_out):
    local_rows = density.shape[0]
    first_row = lax.axis_index("row") * local_rows
    active = active_band(density, mask_band, first_row, local_rows * lax.axis_size("row"))
    own = lax.all_to_all(active.reshape(16, 5 * OWN, 8, BLK), LAYERS, split_axis=0, concat_axis=0, tiled=True)
    up = [(i, i + 1) for i in range(255)]
    down = [(i + 1, i) for i in range(255)]
    to_before = jnp.concatenate([own[:, 0:12], own[:, 15:16]], axis=1)
    to_after = jnp.concatenate([own[:, 4:5], own[:, 8:20]], axis=1)
    before = lax.ppermute(to_after, EVERY, up)
    after = lax.ppermute(to_before, EVERY, down)
    purified = compute(own, after, before, mask_square, mask_out)
    result = lax.all_to_all(purified, LAYERS, split_axis=0, concat_axis=0, tiled=True)
    return result.reshape(density.shape)


def solution(mesh):
    return jax.shard_map(
        on_device,
        mesh=mesh,
        in_specs=(
            P("row", None, ("col", "depth"), None),
            P("row", None),
            P("row", None),
            P("row", None),
        ),
        out_specs=P("row", None, ("col", "depth"), None),
        check_vma=False,
    )
```

```python
import jax
import jax.numpy as jnp
from jax import lax
from jax.experimental import pallas as pl
from jax.experimental.pallas import tpu as pltpu
from jax.sharding import PartitionSpec as P

BLK = 128
OWN = 4
HALO = 4
PAIR = 2 * BLK
LAYERS = ("col", "depth")
EVERY = ("row", "col", "depth")

OUTER = [(row, slot) for row in (0, 3) for slot in range(5)]
INNER = [(row, slot) for row in (1, 2) for slot in range(5)]
OUTER_TO_BEFORE, OUTER_TO_AFTER = slice(0, 6), slice(4, 10)
INNER_TO_BEFORE, INNER_TO_AFTER = slice(0, 7), slice(3, 10)


def put_block(row, slot, value, high, low):
    top = row * BLK
    left = (row + slot - 2) * BLK
    rounded = value.astype(jnp.bfloat16)
    high[top : top + BLK, left : left + BLK] = rounded
    low[top : top + BLK, left : left + BLK] = (value - rounded.astype(jnp.float32)).astype(jnp.bfloat16)


def product(left_high, left_low, right_high, right_low):
    def dot(a, b):
        return jnp.dot(a, b, preferred_element_type=jnp.float32)

    return dot(left_high, right_high) + (dot(left_high, right_low) + dot(left_low, right_high))


def compute_kernel(
    outer, inner, outer_after, inner_after, outer_before, inner_before, weight, square_mask, out_mask, out, high, low, square_high, square_low
):
    first = lax.axis_index(LAYERS) * OWN
    zero = jnp.zeros((BLK, BLK), jnp.bfloat16)
    for pair in range(1, 5):
        for row, column in ((2 * pair + 1, 2 * pair - 2), (2 * pair, 2 * pair + 3)):
            high[row * BLK : (row + 1) * BLK, column * BLK : (column + 1) * BLK] = zero
            low[row * BLK : (row + 1) * BLK, column * BLK : (column + 1) * BLK] = zero
    for row, column in ((0, 3), (11, 8)):
        high[row * BLK : (row + 1) * BLK, column * BLK : (column + 1) * BLK] = zero
        low[row * BLK : (row + 1) * BLK, column * BLK : (column + 1) * BLK] = zero
    for source, blocks, shift in (
        (outer_before, OUTER[OUTER_TO_AFTER], 0),
        (inner_before, INNER[INNER_TO_AFTER], 0),
        (outer_after, OUTER[OUTER_TO_BEFORE], HALO + OWN),
        (inner_after, INNER[INNER_TO_BEFORE], HALO + OWN),
    ):
        for place, (row, slot) in enumerate(blocks):
            put_block(shift + row, slot, source[:, place].reshape(BLK, BLK), high, low)
    for source, blocks in ((outer, OUTER), (inner, INNER)):
        for place, (row, slot) in enumerate(blocks):
            put_block(HALO + row, slot, source[:, place].reshape(BLK, BLK) * weight[row, slot], high, low)

    def tile(low_index, high_index):
        return slice(low_index * PAIR, high_index * PAIR)

    for pair in (2, 3):
        mine = tile(pair, pair + 1)
        kept = {}
        for column in range(pair - 2, pair + 3):
            inner = tile(max(pair, column) - 1, min(pair, column) + 2)
            outer = tile(column, column + 1)
            square = product(high[mine, inner], low[mine, inner], high[inner, outer], low[inner, outer])
            for half in range(2):
                for side in range(2):
                    slot = 2 * (column - pair) + side - half + 4
                    block = square[half * BLK : (half + 1) * BLK, side * BLK : (side + 1) * BLK]
                    row = 2 * (pair - 2) + half
                    if 0 <= slot < 9:
                        block = block * square_mask[first + row, slot].astype(jnp.float32)
                    if 2 <= slot < 7:
                        kept[row, slot - 2] = block
                    rounded = block.astype(jnp.bfloat16)
                    rows = slice(half * BLK, (half + 1) * BLK)
                    columns = slice(column * PAIR + side * BLK, column * PAIR + (side + 1) * BLK)
                    square_high[rows, columns] = rounded
                    square_low[rows, columns] = (block - rounded.astype(jnp.float32)).astype(jnp.bfloat16)
        for column in range(pair - 1, pair + 2):
            inner = tile(column - 1, column + 2)
            outer = tile(column, column + 1)
            cube = product(square_high[:, inner], square_low[:, inner], high[inner, outer], low[inner, outer])
            for half in range(2):
                for side in range(2):
                    slot = 2 * (column - pair) + side - half + 2
                    row = 2 * (pair - 2) + half
                    if 0 <= slot < 5:
                        block = cube[half * BLK : (half + 1) * BLK, side * BLK : (side + 1) * BLK]
                        gate = out_mask[first + row, slot].astype(jnp.float32)
                        block = gate * (3.0 * kept[row, slot] - 2.0 * block)
                        out[:, row * 5 + slot] = block.reshape(16, 8, BLK)


def compute(*operands):
    vmem = pl.BlockSpec(memory_space=pltpu.VMEM)
    smem = pl.BlockSpec(memory_space=pltpu.SMEM)
    window = (OWN + 2 * HALO) * BLK
    return pl.pallas_call(
        compute_kernel,
        out_shape=jax.ShapeDtypeStruct((16, 5 * OWN, 8, BLK), jnp.float32),
        in_specs=[vmem] * 6 + [smem] * 3,
        out_specs=vmem,
        scratch_shapes=[
            pltpu.VMEM((window, window), jnp.bfloat16),
            pltpu.VMEM((window, window), jnp.bfloat16),
            pltpu.VMEM((PAIR, window), jnp.bfloat16),
            pltpu.VMEM((PAIR, window), jnp.bfloat16),
        ],
        compiler_params=pltpu.CompilerParams(vmem_limit_bytes=40 * 1024 * 1024),
        cost_estimate=pl.CostEstimate(flops=2 * 3 * 36 * 256**3, bytes_accessed=6 * 1024 * 1024, transcendentals=0),
    )(*operands)


def swap(value, axis, dim):
    me = lax.axis_index(axis)
    size = lax.axis_size(axis)
    pieces = [lax.dynamic_slice_in_dim(value, me, 1, dim)]
    for k in range(1, size):
        piece = lax.dynamic_slice_in_dim(value, me ^ k, 1, dim)
        pieces.append(lax.ppermute(piece, axis, [(i, i ^ k) for i in range(size)]))
    stack = jnp.concatenate(pieces, axis=dim)
    return jnp.concatenate([lax.dynamic_slice_in_dim(stack, me ^ j, 1, dim) for j in range(size)], axis=dim)


def exchange(col_first, depth_first):
    one = swap(col_first, "col", 0)
    other = swap(depth_first, "depth", 1)
    other = swap(other, "col", 0)
    one = swap(one, "depth", 1)
    return one, other


def shift(value):
    return [(i, i + 1) for i in range(value)], [(i + 1, i) for i in range(value)]


def on_device(density, mask_band, mask_square, mask_out):
    local_rows = density.shape[0]
    total_rows = local_rows * lax.axis_size("row")
    begin = lax.axis_index(LAYERS) * OWN
    rows = lax.axis_index("row") * local_rows + begin + jnp.arange(OWN, dtype=jnp.int32)
    columns = rows[:, None] + jnp.arange(5, dtype=jnp.int32)[None, :] - 2
    inside = ((columns >= 0) & (columns < total_rows)).astype(jnp.float32)
    weight = lax.dynamic_slice_in_dim(mask_band, begin, OWN, 0).astype(jnp.float32) * inside
    groups = density.reshape(4, 4, OWN, 5, 8, BLK)
    inner, outer = exchange(
        groups[:, :, 1:3].reshape(4, 4, 10, 8, BLK), groups[:, :, 0::3].reshape(4, 4, 10, 8, BLK)
    )
    inner = inner.reshape(16, 10, 8, BLK)
    outer = outer.reshape(16, 10, 8, BLK)
    up, down = shift(255)

    def halo(group, group_weight, part, pairs):
        gate = group_weight.reshape(10)[part][None, :, None, None]
        return lax.ppermute(group[:, part] * gate, EVERY, pairs)

    inner_after = halo(inner, weight[1:3], INNER_TO_BEFORE, down)
    inner_before = halo(inner, weight[1:3], INNER_TO_AFTER, up)
    outer_after = halo(outer, weight[0::3], OUTER_TO_BEFORE, down)
    outer_before = halo(outer, weight[0::3], OUTER_TO_AFTER, up)
    purified = compute(
        outer, inner, outer_after, inner_after, outer_before, inner_before, weight, mask_square, mask_out
    )
    purified = purified.reshape(4, 4, 2, 10, 8, BLK)
    lower, upper = exchange(purified[:, :, 0], purified[:, :, 1])
    result = jnp.stack([lower, upper], axis=2)
    return result.reshape(density.shape)


def solution(mesh):
    return jax.shard_map(
        on_device,
        mesh=mesh,
        in_specs=(
            P("row", None, ("col", "depth"), None),
            P("row", None),
            P("row", None),
            P("row", None),
        ),
        out_specs=P("row", None, ("col", "depth"), None),
        check_vma=False,
    )
```

```python
import functools

import jax
import jax.numpy as jnp
from jax import lax
from jax.experimental import pallas as pl
from jax.experimental.pallas import tpu as pltpu
from jax.sharding import PartitionSpec as P

BLK = 128
OWN = 4
HALO = 4
PAIR = 2 * BLK
FIRST_OUT = 8
EVERY = ("row", "col", "depth")

BEFORE_ONLY = [(0, s) for s in range(4)] + [(1, s) for s in range(3)]
BOTH = [(0, 4), (1, 3), (1, 4), (2, 0), (2, 1), (3, 0)]
AFTER_ONLY = [(2, s) for s in range(2, 5)] + [(3, s) for s in range(1, 5)]
EARLY_SIDE = 1
INNER = BEFORE_ONLY[7 - EARLY_SIDE :] + BOTH + AFTER_ONLY[:EARLY_SIDE]
OUTER = BEFORE_ONLY[: 7 - EARLY_SIDE] + AFTER_ONLY[EARLY_SIDE:]
INNER_TO_BEFORE, INNER_TO_AFTER = slice(0, 6 + EARLY_SIDE), slice(EARLY_SIDE, 6 + 2 * EARLY_SIDE)
OUTER_TO_BEFORE, OUTER_TO_AFTER = slice(0, 7 - EARLY_SIDE), slice(7 - EARLY_SIDE, 14 - 2 * EARLY_SIDE)


def ranks(row, col, depth):
    core, z_half = row & 1, (row >> 1) & 1
    return col ^ (3 * (core ^ z_half)), depth ^ (3 * core)


def place():
    return tuple(lax.axis_index(axis) for axis in EVERY)


def pack_kernel(last_row, density, mask, *outs):
    row, col, depth = place()
    col_rank, depth_rank = ranks(row, col, depth)

    def weight(rank, block_row, slot):
        value = mask[slot, rank * OWN + block_row].astype(jnp.float32)
        if block_row + slot < 2:
            value = jnp.where((row == 0) & (rank == 0), 0.0, value)
        if block_row + slot > OWN + 1:
            value = jnp.where((row == last_row) & (rank == 15), 0.0, value)
        return value

    for k in range(4):
        for other in range(4):
            rank = (col_rank ^ k) * 4 + other
            for index, (block_row, slot) in enumerate(INNER):
                outs[k][0, other, index] = density[rank * OWN + block_row, slot] * weight(rank, block_row, slot)
            rank = other * 4 + (depth_rank ^ k)
            for index, (block_row, slot) in enumerate(OUTER):
                outs[4 + k][other, 0, index] = density[rank * OWN + block_row, slot] * weight(rank, block_row, slot)


def pack(density, mask):
    vmem = pl.BlockSpec(memory_space=pltpu.VMEM)
    smem = pl.BlockSpec(memory_space=pltpu.SMEM)
    inner = jax.ShapeDtypeStruct((1, 4, len(INNER), 8, BLK), jnp.float32)
    outer = jax.ShapeDtypeStruct((4, 1, len(OUTER), 8, BLK), jnp.float32)
    outs = pl.pallas_call(
        functools.partial(pack_kernel, lax.axis_size("row") - 1),
        out_shape=[inner] * 4 + [outer] * 4,
        in_specs=[vmem, smem],
        out_specs=[vmem] * 8,
        compiler_params=pltpu.CompilerParams(vmem_limit_bytes=16 * 1024 * 1024),
        cost_estimate=pl.CostEstimate(flops=10**6, bytes_accessed=4 * 1024 * 1024, transcendentals=0),
    )(density, mask)
    return list(outs[:4]), list(outs[4:])


EARLY = (
    [(row, slot) for row, slot in OUTER]
    + [(row, slot) for row, slot in INNER]
    + [(row + OWN, slot) for row, slot in INNER[INNER_TO_BEFORE]]
    + [(row - OWN, slot) for row, slot in INNER[INNER_TO_AFTER]]
)
LATE_AFTER = [(row + OWN, slot) for row, slot in OUTER[OUTER_TO_BEFORE]]
LATE_BEFORE = [(row - OWN, slot) for row, slot in OUTER[OUTER_TO_AFTER]]


def split_block(value):
    rounded = value.astype(jnp.bfloat16)
    return rounded, (value - rounded.astype(jnp.float32)).astype(jnp.bfloat16)


def split_kernel(outer, inner, inner_after, inner_before, high, low):
    index = 0
    for source in (outer, inner, inner_after, inner_before):
        for at in range(source.shape[1]):
            high[index], low[index] = split_block(source[:, at].reshape(BLK, BLK))
            index += 1


def split(*operands):
    vmem = pl.BlockSpec(memory_space=pltpu.VMEM)
    part = jax.ShapeDtypeStruct((len(EARLY), BLK, BLK), jnp.bfloat16)
    return pl.pallas_call(
        split_kernel,
        out_shape=(part, part),
        in_specs=[vmem] * 4,
        out_specs=(vmem, vmem),
        cost_estimate=pl.CostEstimate(flops=0, bytes_accessed=16 * 1024 * 1024, transcendentals=0),
        compiler_params=pltpu.CompilerParams(vmem_limit_bytes=16 * 1024 * 1024),
    )(*operands)


def put_block(row, column, parts, high, low):
    rows, columns = slice(row * BLK, (row + 1) * BLK), slice(column * BLK, (column + 1) * BLK)
    high[rows, columns], low[rows, columns] = parts


def product(left_high, left_low, right_high, right_low):
    def dot(a, b):
        return jnp.dot(a, b, preferred_element_type=jnp.float32)

    return dot(left_high, right_high) + (dot(left_high, right_low) + dot(left_low, right_high))


def tile(first, end):
    return slice(first * PAIR, end * PAIR)


def compute_kernel(top, early_high, early_low, late_after, late_before, square_mask, out_mask, *refs):
    *outs, high, low, square_high, square_low = refs
    col_rank, depth_rank = ranks(*place())
    first = (col_rank * 4 + depth_rank) * OWN + top
    zero = jnp.zeros((BLK, BLK), jnp.bfloat16)
    for row, column in ((3, 0), (2, 5), (5, 2), (4, 7), (7, 4), (6, 9), (0, 3), (9, 6)):
        high[row * BLK : (row + 1) * BLK, column * BLK : (column + 1) * BLK] = zero
        low[row * BLK : (row + 1) * BLK, column * BLK : (column + 1) * BLK] = zero
    def needed(blocks):
        for index, (row, slot) in enumerate(blocks):
            at = row - top + 4
            column = at + slot - 2
            if 2 <= at < 8 or (0 <= at < 2 and 2 <= column < 4) or (8 <= at < 10 and 6 <= column < 8):
                yield index, at, column

    for index, row, column in needed(EARLY):
        put_block(row, column, (early_high[index], early_low[index]), high, low)
    for source, blocks in ((late_after, LATE_AFTER), (late_before, LATE_BEFORE)):
        for index, row, column in needed(blocks):
            put_block(row, column, split_block(source[:, index].reshape(BLK, BLK)), high, low)

    kept = {}
    for column in range(5):
        inside, outside = tile(max(2, column) - 1, min(2, column) + 2), tile(column, column + 1)
        square = product(high[tile(2, 3), inside], low[tile(2, 3), inside], high[inside, outside], low[inside, outside])
        for half in range(2):
            for side in range(2):
                slot = 2 * column + side - half
                block = square[half * BLK : (half + 1) * BLK, side * BLK : (side + 1) * BLK]
                if 0 <= slot < 9:
                    block = block * square_mask[slot, first + half].astype(jnp.float32)
                if 2 <= slot < 7:
                    kept[half, slot - 2] = block
                put_block(half, 2 * column + side, split_block(block), square_high, square_low)
    for column in range(1, 4):
        inside, outside = tile(column - 1, column + 2), tile(column, column + 1)
        cube = product(square_high[:, inside], square_low[:, inside], high[inside, outside], low[inside, outside])
        for half in range(2):
            for side in range(2):
                slot = 2 * column + side - half - 2
                if 0 <= slot < 5:
                    block = cube[half * BLK : (half + 1) * BLK, side * BLK : (side + 1) * BLK]
                    gate = out_mask[slot, first + half].astype(jnp.float32)
                    value = (gate * (3.0 * kept[half, slot] - 2.0 * block)).reshape(16, 8, BLK)
                    index = half * 5 + slot
                    if index < outs[0].shape[1]:
                        outs[0][:, index] = value
                    else:
                        outs[1][:, index - outs[0].shape[1]] = value


def compute(top, counts, *operands):
    vmem = pl.BlockSpec(memory_space=pltpu.VMEM)
    smem = pl.BlockSpec(memory_space=pltpu.SMEM)
    window = 10 * BLK
    return pl.pallas_call(
        functools.partial(compute_kernel, top),
        out_shape=[jax.ShapeDtypeStruct((16, count, 8, BLK), jnp.float32) for count in counts],
        in_specs=[vmem] * 4 + [smem] * 2,
        out_specs=[vmem] * len(counts),
        scratch_shapes=[
            pltpu.VMEM((window, window), jnp.bfloat16),
            pltpu.VMEM((window, window), jnp.bfloat16),
            pltpu.VMEM((PAIR, window), jnp.bfloat16),
            pltpu.VMEM((PAIR, window), jnp.bfloat16),
        ],
        compiler_params=pltpu.CompilerParams(vmem_limit_bytes=32 * 1024 * 1024),
        cost_estimate=pl.CostEstimate(flops=2 * 3 * 18 * 256**3, bytes_accessed=4 * 1024 * 1024, transcendentals=0),
    )(*operands)


def send(pieces, axis):
    size = lax.axis_size(axis)
    return pieces[:1] + [lax.ppermute(pieces[k], axis, [(i, i ^ k) for i in range(size)]) for k in range(1, size)]


def cut(value, dim, far):
    return [lax.dynamic_slice_in_dim(value, far ^ k, 1, dim) for k in range(value.shape[dim])]


def join(pieces, dim, near):
    stack = jnp.concatenate(pieces, axis=dim)
    return jnp.concatenate([lax.dynamic_slice_in_dim(stack, near ^ j, 1, dim) for j in range(len(pieces))], axis=dim)


def swap(value, axis, dim, near, far):
    return join(send(cut(value, dim, far), axis), dim, near)


def chain(rows):
    places = [(row, col, depth) for row in range(rows) for col in range(4) for depth in range(4)]
    places.sort(key=lambda at: (at[0], *ranks(*at)))
    return [row * 16 + col * 4 + depth for row, col, depth in places]


def on_device(density, mask_band, mask_square, mask_out):
    row, col, depth = place()
    col_rank, depth_rank = ranks(row, col, depth)
    order = chain(lax.axis_size("row"))
    up = list(zip(order[:-1], order[1:]))
    down = list(zip(order[1:], order[:-1]))

    def halo(group, before_part, after_part):
        after = lax.ppermute(group[:, before_part], EVERY, down)
        before = lax.ppermute(group[:, after_part], EVERY, up)
        return after, before

    inner, outer = pack(density, mask_band.T)
    inner = join(send(inner, "col"), 0, col)
    outer = join(send(outer, "depth"), 1, depth)
    outer = swap(outer, "col", 0, col, col_rank)
    inner = swap(inner, "depth", 1, depth, depth_rank)
    inner = inner.reshape(16, len(INNER), 8, BLK)
    outer = outer.reshape(16, len(OUTER), 8, BLK)
    early = split(outer, inner, *halo(inner, INNER_TO_BEFORE, INNER_TO_AFTER))
    operands = (*early, *halo(outer, OUTER_TO_BEFORE, OUTER_TO_AFTER), mask_square.T, mask_out.T)
    lower, middle = compute(0, (FIRST_OUT, 10 - FIRST_OUT), *operands)
    lower, operands = lax.optimization_barrier((lower, operands))
    (upper,) = compute(2, (10,), *operands)
    upper = jnp.concatenate([middle, upper], axis=1)
    lower = lower.reshape(4, 4, FIRST_OUT, 8, BLK)
    upper = upper.reshape(4, 4, 20 - FIRST_OUT, 8, BLK)
    lower = swap(lower, "col", 0, col_rank, col)
    upper = swap(upper, "depth", 1, depth_rank, depth)
    upper = send(cut(upper, 0, col), "col")
    upper[1], lower = lax.optimization_barrier((upper[1], lower))
    upper = join(upper, 0, col_rank)
    lower = swap(lower, "depth", 1, depth_rank, depth)
    return jnp.concatenate([lower, upper], axis=2).reshape(density.shape)


def solution(mesh):
    return jax.shard_map(
        on_device,
        mesh=mesh,
        in_specs=(
            P("row", None, ("col", "depth"), None),
            P("row", None),
            P("row", None),
            P("row", None),
        ),
        out_specs=P("row", None, ("col", "depth"), None),
        check_vma=False,
    )
```

```python
import functools

import jax
import jax.numpy as jnp
from jax import lax
from jax.experimental import pallas as pl
from jax.experimental.pallas import tpu as pltpu
from jax.sharding import PartitionSpec as P

BLK = 128
OWN = 4
HALO = 4
PAIR = 2 * BLK
FIRST_OUT = 9
EVERY = ("row", "col", "depth")

BEFORE_ONLY = [(0, s) for s in range(4)] + [(1, s) for s in range(3)]
BOTH = [(0, 4), (1, 3), (1, 4), (2, 0), (2, 1), (3, 0)]
AFTER_ONLY = [(2, s) for s in range(2, 5)] + [(3, s) for s in range(1, 5)]
EARLY_SIDE = 1
INNER = BEFORE_ONLY[7 - EARLY_SIDE :] + BOTH + AFTER_ONLY[:EARLY_SIDE]
OUTER = BEFORE_ONLY[: 7 - EARLY_SIDE] + AFTER_ONLY[EARLY_SIDE:]
INNER_TO_BEFORE, INNER_TO_AFTER = slice(0, 6 + EARLY_SIDE), slice(EARLY_SIDE, 6 + 2 * EARLY_SIDE)
OUTER_TO_BEFORE, OUTER_TO_AFTER = slice(0, 7 - EARLY_SIDE), slice(7 - EARLY_SIDE, 14 - 2 * EARLY_SIDE)


def ranks(row, col, depth):
    core, z_half = row & 1, (row >> 1) & 1
    return col ^ (3 * (core ^ z_half)), depth ^ (3 * core)


def place():
    return tuple(lax.axis_index(axis) for axis in EVERY)


def pack_kernel(last_row, density, mask, *outs):
    row, col, depth = place()
    col_rank, depth_rank = ranks(row, col, depth)

    def weight(rank, block_row, slot):
        value = mask[slot, rank * OWN + block_row].astype(jnp.float32)
        if block_row + slot < 2:
            value = jnp.where((row == 0) & (rank == 0), 0.0, value)
        if block_row + slot > OWN + 1:
            value = jnp.where((row == last_row) & (rank == 15), 0.0, value)
        return value

    for k in range(4):
        for other in range(4):
            rank = (col_rank ^ k) * 4 + other
            for index, (block_row, slot) in enumerate(INNER):
                outs[k][0, other, index] = density[rank * OWN + block_row, slot] * weight(rank, block_row, slot)
            rank = other * 4 + (depth_rank ^ k)
            for index, (block_row, slot) in enumerate(OUTER):
                outs[4 + k][other, 0, index] = density[rank * OWN + block_row, slot] * weight(rank, block_row, slot)


def pack(density, mask):
    vmem = pl.BlockSpec(memory_space=pltpu.VMEM)
    smem = pl.BlockSpec(memory_space=pltpu.SMEM)
    inner = jax.ShapeDtypeStruct((1, 4, len(INNER), 8, BLK), jnp.float32)
    outer = jax.ShapeDtypeStruct((4, 1, len(OUTER), 8, BLK), jnp.float32)
    outs = pl.pallas_call(
        functools.partial(pack_kernel, lax.axis_size("row") - 1),
        out_shape=[inner] * 4 + [outer] * 4,
        in_specs=[vmem, smem],
        out_specs=[vmem] * 8,
        compiler_params=pltpu.CompilerParams(vmem_limit_bytes=16 * 1024 * 1024),
        cost_estimate=pl.CostEstimate(flops=10**6, bytes_accessed=4 * 1024 * 1024, transcendentals=0),
    )(density, mask)
    return list(outs[:4]), list(outs[4:])


EARLY_AFTER = [(row + OWN, slot) for row, slot in INNER[INNER_TO_BEFORE]]
EARLY_BEFORE = [(row - OWN, slot) for row, slot in INNER[INNER_TO_AFTER]]
LATE_AFTER = [(row + OWN, slot) for row, slot in OUTER[OUTER_TO_BEFORE]]
LATE_BEFORE = [(row - OWN, slot) for row, slot in OUTER[OUTER_TO_AFTER]]
TILES = [(0, 1), (5, 4)] + [(pair, column) for pair in range(1, 5) for column in range(pair - 1, pair + 2)]
MINE = (2, 3)


def at(row, slot):
    return row + 4, row + slot + 2


def split_block(value):
    rounded = value.astype(jnp.bfloat16)
    return rounded, (value - rounded.astype(jnp.float32)).astype(jnp.bfloat16)


def put_block(row, column, parts, high, low):
    rows, columns = slice(row * BLK, (row + 1) * BLK), slice(column * BLK, (column + 1) * BLK)
    high[rows, columns], low[rows, columns] = parts


def product(left_high, left_low, right_high, right_low):
    def dot(a, b):
        return jnp.dot(a, b, preferred_element_type=jnp.float32)

    return dot(left_high, right_high) + (dot(left_high, right_low) + dot(left_low, right_high))


def tile(first, end):
    return slice(first * PAIR, end * PAIR)


def early_kernel(outer, inner, inner_after, inner_before, high, low, square):
    there = set()
    for source, blocks in ((outer, OUTER), (inner, INNER), (inner_after, EARLY_AFTER), (inner_before, EARLY_BEFORE)):
        for index, block in enumerate(blocks):
            put_block(*at(*block), split_block(source[:, index].reshape(BLK, BLK)), high, low)
            there.add(at(*block))
    zero = jnp.zeros((BLK, BLK), jnp.bfloat16)
    for pair, outside in TILES:
        for row in (2 * pair, 2 * pair + 1):
            for column in (2 * outside, 2 * outside + 1):
                if (row, column) not in there:
                    put_block(row, column, (zero, zero), high, low)
    for pair in MINE:
        mine = tile(pair, pair + 1)
        for column in range(pair - 2, pair + 3):
            inside, outside = tile(max(pair, column) - 1, min(pair, column) + 2), tile(column, column + 1)
            square[pair - MINE[0], :, tile(column - pair + 2, column - pair + 3)] = product(
                high[mine, inside], low[mine, inside], high[inside, outside], low[inside, outside]
            )


def early_part(*operands):
    vmem = pl.BlockSpec(memory_space=pltpu.VMEM)
    window = 12 * BLK
    part = jax.ShapeDtypeStruct((window, window), jnp.bfloat16)
    return pl.pallas_call(
        early_kernel,
        out_shape=(part, part, jax.ShapeDtypeStruct((2, PAIR, 5 * PAIR), jnp.float32)),
        in_specs=[vmem] * 4,
        out_specs=(vmem, vmem, vmem),
        compiler_params=pltpu.CompilerParams(vmem_limit_bytes=24 * 1024 * 1024),
        cost_estimate=pl.CostEstimate(flops=2 * 3 * 18 * PAIR**3, bytes_accessed=16 * 1024 * 1024, transcendentals=0),
    )(*operands)


def late_kernel(after, before, high_in, low_in, square, square_mask, out_mask, *refs):
    *outs, high, low, late_high, late_low, square_high, square_low = refs
    col_rank, depth_rank = ranks(*place())
    first = (col_rank * 4 + depth_rank) * OWN
    late = {}
    for side, (source, blocks) in enumerate(((before, LATE_BEFORE), (after, LATE_AFTER))):
        there = set()
        pair = 1 + 3 * side
        for index, block in enumerate(blocks):
            row, column = at(*block)
            parts = split_block(source[:, index].reshape(BLK, BLK))
            put_block(row, column, parts, high, low)
            put_block(2 * side + row - 2 * pair, column - 2 * pair + 2, parts, late_high, late_low)
            there.add((row, column))
        zero = jnp.zeros((BLK, BLK), jnp.bfloat16)
        late[pair + 1 - 2 * side] = (pair, side, {column // 2 for _, column in there})
        for row in (2 * pair, 2 * pair + 1):
            for column in range(2 * pair - 2, 2 * pair + 4):
                if (row, column) not in there:
                    put_block(2 * side + row - 2 * pair, column - 2 * pair + 2, (zero, zero), late_high, late_low)
    for pair in MINE:
        mine = tile(pair, pair + 1)
        kept = {}
        source, side, touched = late[pair]
        for column in range(pair - 2, pair + 3):
            value = square[pair - MINE[0], :, tile(column - pair + 2, column - pair + 3)]
            if column in touched:
                inside, rows, outside = tile(source, source + 1), tile(side, side + 1), tile(column - source + 1, column - source + 2)
                value += product(high[mine, inside], low[mine, inside], late_high[rows, outside], late_low[rows, outside])
            for half in range(2):
                for part in range(2):
                    slot = 2 * (column - pair) + part - half + 4
                    block = value[half * BLK : (half + 1) * BLK, part * BLK : (part + 1) * BLK]
                    row = 2 * (pair - MINE[0]) + half
                    if 0 <= slot < 9:
                        block = block * square_mask[slot, first + row].astype(jnp.float32)
                    if 2 <= slot < 7:
                        kept[half, slot - 2] = block
                    put_block(half, 2 * column + part, split_block(block), square_high, square_low)
        for column in range(pair - 1, pair + 2):
            inside, outside = tile(column - 1, column + 2), tile(column, column + 1)
            cube = product(square_high[:, inside], square_low[:, inside], high[inside, outside], low[inside, outside])
            for half in range(2):
                for part in range(2):
                    slot = 2 * (column - pair) + part - half + 2
                    row = 2 * (pair - MINE[0]) + half
                    if 0 <= slot < 5:
                        block = cube[half * BLK : (half + 1) * BLK, part * BLK : (part + 1) * BLK]
                        gate = out_mask[slot, first + row].astype(jnp.float32)
                        value = (gate * (3.0 * kept[half, slot] - 2.0 * block)).reshape(16, 8, BLK)
                        index = row * 5 + slot
                        if index < FIRST_OUT:
                            outs[0][:, index] = value
                        else:
                            outs[1][:, index - FIRST_OUT] = value


def late_part(*operands):
    vmem = pl.BlockSpec(memory_space=pltpu.VMEM)
    smem = pl.BlockSpec(memory_space=pltpu.SMEM)
    window = 12 * BLK
    part = jax.ShapeDtypeStruct((window, window), jnp.bfloat16)
    return pl.pallas_call(
        late_kernel,
        out_shape=[jax.ShapeDtypeStruct((16, count, 8, BLK), jnp.float32) for count in (FIRST_OUT, 20 - FIRST_OUT)] + [part] * 2,
        in_specs=[vmem] * 5 + [smem] * 2,
        out_specs=[vmem] * 4,
        scratch_shapes=[pltpu.VMEM((2 * PAIR, 3 * PAIR), jnp.bfloat16)] * 2 + [pltpu.VMEM((PAIR, window), jnp.bfloat16)] * 2,
        input_output_aliases={2: 2, 3: 3},
        compiler_params=pltpu.CompilerParams(vmem_limit_bytes=24 * 1024 * 1024),
        cost_estimate=pl.CostEstimate(flops=2 * 3 * 22 * PAIR**3, bytes_accessed=4 * 1024 * 1024, transcendentals=0),
    )(*operands)[:2]


def send(pieces, axis):
    size = lax.axis_size(axis)
    return pieces[:1] + [lax.ppermute(pieces[k], axis, [(i, i ^ k) for i in range(size)]) for k in range(1, size)]


def cut(value, dim, far):
    return [lax.dynamic_slice_in_dim(value, far ^ k, 1, dim) for k in range(value.shape[dim])]


def join(pieces, dim, near):
    stack = jnp.concatenate(pieces[::-1], axis=dim)
    last = len(pieces) - 1
    return jnp.concatenate([lax.dynamic_slice_in_dim(stack, near ^ j ^ last, 1, dim) for j in range(len(pieces))], axis=dim)


def swap(value, axis, dim, near, far):
    return join(send(cut(value, dim, far), axis), dim, near)


def chain(rows):
    places = [(row, col, depth) for row in range(rows) for col in range(4) for depth in range(4)]
    places.sort(key=lambda at: (at[0], *ranks(*at)))
    return [row * 16 + col * 4 + depth for row, col, depth in places]


def on_device(density, mask_band, mask_square, mask_out):
    row, col, depth = place()
    col_rank, depth_rank = ranks(row, col, depth)
    order = chain(lax.axis_size("row"))
    up = list(zip(order[:-1], order[1:]))
    down = list(zip(order[1:], order[:-1]))

    def halo(group, before_part, after_part):
        after = lax.ppermute(group[:, before_part], EVERY, down)
        before = lax.ppermute(group[:, after_part], EVERY, up)
        return after, before

    inner, outer = pack(density, mask_band.T)
    inner = join(send(inner, "col"), 0, col)
    outer = join(send(outer, "depth"), 1, depth)
    outer = swap(outer, "col", 0, col, col_rank)
    inner = swap(inner, "depth", 1, depth, depth_rank)
    inner = inner.reshape(16, len(INNER), 8, BLK)
    outer = outer.reshape(16, len(OUTER), 8, BLK)
    early = early_part(outer, inner, *halo(inner, INNER_TO_BEFORE, INNER_TO_AFTER))
    late = halo(outer, OUTER_TO_BEFORE, OUTER_TO_AFTER)
    lower, upper = late_part(*late, *early, mask_square.T, mask_out.T)
    lower = lower.reshape(4, 4, FIRST_OUT, 8, BLK)
    upper = upper.reshape(4, 4, 20 - FIRST_OUT, 8, BLK)
    lower = swap(lower, "col", 0, col_rank, col)
    upper = swap(upper, "depth", 1, depth_rank, depth)
    upper = send(cut(upper, 0, col), "col")
    upper[1], lower = lax.optimization_barrier((upper[1], lower))
    upper = join(upper, 0, col_rank)
    lower = swap(lower, "depth", 1, depth_rank, depth)
    return jnp.concatenate([lower, upper], axis=2).reshape(density.shape)


def solution(mesh):
    return jax.shard_map(
        on_device,
        mesh=mesh,
        in_specs=(
            P("row", None, ("col", "depth"), None),
            P("row", None),
            P("row", None),
            P("row", None),
        ),
        out_specs=P("row", None, ("col", "depth"), None),
        check_vma=False,
    )
```

```python
import functools

import jax
import jax.numpy as jnp
from jax import lax
from jax.experimental import pallas as pl
from jax.experimental.pallas import tpu as pltpu
from jax.sharding import PartitionSpec as P

BLK = 128
OWN = 4
HALO = 4
PAIR = 2 * BLK
FIRST_OUT = 9
EVERY = ("row", "col", "depth")

BEFORE_ONLY = [(0, s) for s in range(4)] + [(1, s) for s in range(3)]
BOTH = [(0, 4), (1, 3), (1, 4), (2, 0), (2, 1), (3, 0)]
AFTER_ONLY = [(2, s) for s in range(2, 5)] + [(3, s) for s in range(1, 5)]
EARLY_SIDE = 1
INNER = BEFORE_ONLY[7 - EARLY_SIDE :] + BOTH + AFTER_ONLY[:EARLY_SIDE]
OUTER = BEFORE_ONLY[: 7 - EARLY_SIDE] + AFTER_ONLY[EARLY_SIDE:]
INNER_TO_BEFORE, INNER_TO_AFTER = slice(0, 6 + EARLY_SIDE), slice(EARLY_SIDE, 6 + 2 * EARLY_SIDE)
OUTER_TO_BEFORE, OUTER_TO_AFTER = slice(0, 7 - EARLY_SIDE), slice(7 - EARLY_SIDE, 14 - 2 * EARLY_SIDE)


def ranks(row, col, depth):
    core, z_half = row & 1, (row >> 1) & 1
    col_rank = col ^ (3 * (core ^ z_half))
    return col_rank, depth ^ (3 * (col_rank & 1))


def place():
    return tuple(lax.axis_index(axis) for axis in EVERY)


def pack_kernel(last_row, density, mask, *outs):
    row, col, depth = place()
    col_rank, depth_rank = ranks(row, col, depth)

    def weight(rank, block_row, slot):
        value = mask[slot, rank * OWN + block_row].astype(jnp.float32)
        if block_row + slot < 2:
            value = jnp.where((row == 0) & (rank == 0), 0.0, value)
        if block_row + slot > OWN + 1:
            value = jnp.where((row == last_row) & (rank == 15), 0.0, value)
        return value

    for k in range(4):
        for other in range(4):
            rank = (col_rank ^ k) * 4 + other
            for index, (block_row, slot) in enumerate(INNER):
                outs[k][0, other, index] = density[rank * OWN + block_row, slot] * weight(rank, block_row, slot)
            rank = other * 4 + (depth ^ (3 * (other & 1)) ^ k)
            for index, (block_row, slot) in enumerate(OUTER):
                outs[4 + k][other, 0, index] = density[rank * OWN + block_row, slot] * weight(rank, block_row, slot)


def pack(density, mask):
    vmem = pl.BlockSpec(memory_space=pltpu.VMEM)
    smem = pl.BlockSpec(memory_space=pltpu.SMEM)
    inner = jax.ShapeDtypeStruct((1, 4, len(INNER), 8, BLK), jnp.float32)
    outer = jax.ShapeDtypeStruct((4, 1, len(OUTER), 8, BLK), jnp.float32)
    outs = pl.pallas_call(
        functools.partial(pack_kernel, lax.axis_size("row") - 1),
        out_shape=[inner] * 4 + [outer] * 4,
        in_specs=[vmem, smem],
        out_specs=[vmem] * 8,
        compiler_params=pltpu.CompilerParams(vmem_limit_bytes=16 * 1024 * 1024),
        cost_estimate=pl.CostEstimate(flops=10**6, bytes_accessed=4 * 1024 * 1024, transcendentals=0),
    )(density, mask)
    return list(outs[:4]), list(outs[4:])


EARLY_AFTER = [(row + OWN, slot) for row, slot in INNER[INNER_TO_BEFORE]]
EARLY_BEFORE = [(row - OWN, slot) for row, slot in INNER[INNER_TO_AFTER]]
LATE_AFTER = [(row + OWN, slot) for row, slot in OUTER[OUTER_TO_BEFORE]]
LATE_BEFORE = [(row - OWN, slot) for row, slot in OUTER[OUTER_TO_AFTER]]
TILES = [(0, 1), (5, 4)] + [(pair, column) for pair in range(1, 5) for column in range(pair - 1, pair + 2)]
MINE = (2, 3)


def at(row, slot):
    return row + 4, row + slot + 2


def split_block(value):
    rounded = value.astype(jnp.bfloat16)
    return rounded, (value - rounded.astype(jnp.float32)).astype(jnp.bfloat16)


def put_block(row, column, parts, high, low):
    rows, columns = slice(row * BLK, (row + 1) * BLK), slice(column * BLK, (column + 1) * BLK)
    high[rows, columns], low[rows, columns] = parts


def product(left_high, left_low, right_high, right_low):
    def dot(a, b):
        return jnp.dot(a, b, preferred_element_type=jnp.float32)

    return dot(left_high, right_high) + (dot(left_high, right_low) + dot(left_low, right_high))


def tile(first, end):
    return slice(first * PAIR, end * PAIR)


def early_kernel(outer, inner, inner_after, inner_before, high, low, square):
    there = set()
    for source, blocks in ((outer, OUTER), (inner, INNER), (inner_after, EARLY_AFTER), (inner_before, EARLY_BEFORE)):
        for index, block in enumerate(blocks):
            put_block(*at(*block), split_block(source[:, index].reshape(BLK, BLK)), high, low)
            there.add(at(*block))
    zero = jnp.zeros((BLK, BLK), jnp.bfloat16)
    for pair, outside in TILES:
        for row in (2 * pair, 2 * pair + 1):
            for column in (2 * outside, 2 * outside + 1):
                if (row, column) not in there:
                    put_block(row, column, (zero, zero), high, low)
    for pair in MINE:
        mine = tile(pair, pair + 1)
        for column in range(pair - 2, pair + 3):
            inside, outside = tile(max(pair, column) - 1, min(pair, column) + 2), tile(column, column + 1)
            square[pair - MINE[0], :, tile(column - pair + 2, column - pair + 3)] = product(
                high[mine, inside], low[mine, inside], high[inside, outside], low[inside, outside]
            )


def early_part(*operands):
    vmem = pl.BlockSpec(memory_space=pltpu.VMEM)
    window = 12 * BLK
    part = jax.ShapeDtypeStruct((window, window), jnp.bfloat16)
    return pl.pallas_call(
        early_kernel,
        out_shape=(part, part, jax.ShapeDtypeStruct((2, PAIR, 5 * PAIR), jnp.float32)),
        in_specs=[vmem] * 4,
        out_specs=(vmem, vmem, vmem),
        compiler_params=pltpu.CompilerParams(vmem_limit_bytes=24 * 1024 * 1024),
        cost_estimate=pl.CostEstimate(flops=2 * 3 * 18 * PAIR**3, bytes_accessed=16 * 1024 * 1024, transcendentals=0),
    )(*operands)


def late_kernel(after, before, high_in, low_in, square, square_mask, out_mask, *refs):
    *outs, high, low, late_high, late_low, square_high, square_low = refs
    col_rank, depth_rank = ranks(*place())
    first = (col_rank * 4 + depth_rank) * OWN
    late = {}
    for side, (source, blocks) in enumerate(((before, LATE_BEFORE), (after, LATE_AFTER))):
        there = set()
        pair = 1 + 3 * side
        for index, block in enumerate(blocks):
            row, column = at(*block)
            parts = split_block(source[:, index].reshape(BLK, BLK))
            put_block(row, column, parts, high, low)
            put_block(2 * side + row - 2 * pair, column - 2 * pair + 2, parts, late_high, late_low)
            there.add((row, column))
        zero = jnp.zeros((BLK, BLK), jnp.bfloat16)
        late[pair + 1 - 2 * side] = (pair, side, {column // 2 for _, column in there})
        for row in (2 * pair, 2 * pair + 1):
            for column in range(2 * pair - 2, 2 * pair + 4):
                if (row, column) not in there:
                    put_block(2 * side + row - 2 * pair, column - 2 * pair + 2, (zero, zero), late_high, late_low)
    for pair in MINE:
        mine = tile(pair, pair + 1)
        kept = {}
        source, side, touched = late[pair]
        for column in range(pair - 2, pair + 3):
            value = square[pair - MINE[0], :, tile(column - pair + 2, column - pair + 3)]
            if column in touched:
                inside, rows, outside = tile(source, source + 1), tile(side, side + 1), tile(column - source + 1, column - source + 2)
                value += product(high[mine, inside], low[mine, inside], late_high[rows, outside], late_low[rows, outside])
            for half in range(2):
                for part in range(2):
                    slot = 2 * (column - pair) + part - half + 4
                    block = value[half * BLK : (half + 1) * BLK, part * BLK : (part + 1) * BLK]
                    row = 2 * (pair - MINE[0]) + half
                    if 0 <= slot < 9:
                        block = block * square_mask[slot, first + row].astype(jnp.float32)
                    if 2 <= slot < 7:
                        kept[half, slot - 2] = block
                    put_block(half, 2 * column + part, split_block(block), square_high, square_low)
        for column in range(pair - 1, pair + 2):
            inside, outside = tile(column - 1, column + 2), tile(column, column + 1)
            cube = product(square_high[:, inside], square_low[:, inside], high[inside, outside], low[inside, outside])
            for half in range(2):
                for part in range(2):
                    slot = 2 * (column - pair) + part - half + 2
                    row = 2 * (pair - MINE[0]) + half
                    if 0 <= slot < 5:
                        block = cube[half * BLK : (half + 1) * BLK, part * BLK : (part + 1) * BLK]
                        gate = out_mask[slot, first + row].astype(jnp.float32)
                        value = (gate * (3.0 * kept[half, slot] - 2.0 * block)).reshape(16, 8, BLK)
                        index = row * 5 + slot
                        if index < FIRST_OUT:
                            outs[0][:, index] = value
                        else:
                            outs[1][:, index - FIRST_OUT] = value


def late_part(*operands):
    vmem = pl.BlockSpec(memory_space=pltpu.VMEM)
    smem = pl.BlockSpec(memory_space=pltpu.SMEM)
    window = 12 * BLK
    part = jax.ShapeDtypeStruct((window, window), jnp.bfloat16)
    return pl.pallas_call(
        late_kernel,
        out_shape=[jax.ShapeDtypeStruct((16, count, 8, BLK), jnp.float32) for count in (FIRST_OUT, 20 - FIRST_OUT)] + [part] * 2,
        in_specs=[vmem] * 5 + [smem] * 2,
        out_specs=[vmem] * 4,
        scratch_shapes=[pltpu.VMEM((2 * PAIR, 3 * PAIR), jnp.bfloat16)] * 2 + [pltpu.VMEM((PAIR, window), jnp.bfloat16)] * 2,
        input_output_aliases={2: 2, 3: 3},
        compiler_params=pltpu.CompilerParams(vmem_limit_bytes=24 * 1024 * 1024),
        cost_estimate=pl.CostEstimate(flops=2 * 3 * 22 * PAIR**3, bytes_accessed=4 * 1024 * 1024, transcendentals=0),
    )(*operands)[:2]


def send(pieces, axis):
    size = lax.axis_size(axis)
    return pieces[:1] + [lax.ppermute(pieces[k], axis, [(i, i ^ k) for i in range(size)]) for k in range(1, size)]


def cut(value, dim, far):
    return [lax.dynamic_slice_in_dim(value, far ^ k, 1, dim) for k in range(value.shape[dim])]


def join(pieces, dim, near):
    stack = jnp.concatenate(pieces[::-1], axis=dim)
    last = len(pieces) - 1
    return jnp.concatenate([lax.dynamic_slice_in_dim(stack, near ^ j ^ last, 1, dim) for j in range(len(pieces))], axis=dim)


def swap(value, axis, dim, near, far):
    return join(send(cut(value, dim, far), axis), dim, near)


def chain(rows):
    places = [(row, col, depth) for row in range(rows) for col in range(4) for depth in range(4)]
    places.sort(key=lambda at: (at[0], *ranks(*at)))
    return [row * 16 + col * 4 + depth for row, col, depth in places]


def on_device(density, mask_band, mask_square, mask_out):
    row, col, depth = place()
    col_rank, depth_rank = ranks(row, col, depth)
    order = chain(lax.axis_size("row"))
    up = list(zip(order[:-1], order[1:]))
    down = list(zip(order[1:], order[:-1]))

    def halo(group, before_part, after_part):
        after = lax.ppermute(group[:, before_part], EVERY, down)
        before = lax.ppermute(group[:, after_part], EVERY, up)
        return after, before

    inner, outer = pack(density, mask_band.T)
    inner = join(send(inner, "col"), 0, col)
    outer = join(send(outer, "depth"), 1, depth)
    outer = swap(outer, "col", 0, col, col_rank)
    inner = swap(inner, "depth", 1, depth, depth_rank)
    inner = inner.reshape(16, len(INNER), 8, BLK)
    outer = outer.reshape(16, len(OUTER), 8, BLK)
    early = early_part(outer, inner, *halo(inner, INNER_TO_BEFORE, INNER_TO_AFTER))
    late = halo(outer, OUTER_TO_BEFORE, OUTER_TO_AFTER)
    lower, upper = late_part(*late, *early, mask_square.T, mask_out.T)
    lower = lower.reshape(4, 4, FIRST_OUT, 8, BLK)
    upper = upper.reshape(4, 4, 20 - FIRST_OUT, 8, BLK)
    lower = swap(lower, "col", 0, col_rank, col)
    upper = swap(upper, "depth", 1, depth_rank, depth)
    upper = send(cut(upper, 0, col), "col")
    upper[1], lower = lax.optimization_barrier((upper[1], lower))
    upper = join(upper, 0, col_rank)
    lower = send(cut(lower, 1, depth), "depth")
    turns = [join([piece[turn::2] for piece in lower], 1, depth ^ (3 * turn)) for turn in range(2)]
    lower = jnp.stack(turns, axis=1).reshape(4, 4, FIRST_OUT, 8, BLK)
    return jnp.concatenate([lower, upper], axis=2).reshape(density.shape)


def solution(mesh):
    return jax.shard_map(
        on_device,
        mesh=mesh,
        in_specs=(
            P("row", None, ("col", "depth"), None),
            P("row", None),
            P("row", None),
            P("row", None),
        ),
        out_specs=P("row", None, ("col", "depth"), None),
        check_vma=False,
    )
```

```python
import functools

import jax
import jax.numpy as jnp
from jax import lax
from jax.experimental import pallas as pl
from jax.experimental.pallas import tpu as pltpu
from jax.sharding import PartitionSpec as P

BLK = 128
OWN = 4
HALO = 4
PAIR = 2 * BLK
FIRST_OUT = 9
EVERY = ("row", "col", "depth")

BEFORE_ONLY = [(0, s) for s in range(4)] + [(1, s) for s in range(3)]
BOTH = [(0, 4), (1, 3), (1, 4), (2, 0), (2, 1), (3, 0)]
AFTER_ONLY = [(2, s) for s in range(2, 5)] + [(3, s) for s in range(1, 5)]
EARLY_SIDE = 1
INNER = BEFORE_ONLY[7 - EARLY_SIDE :] + BOTH + AFTER_ONLY[:EARLY_SIDE]
OUTER = BEFORE_ONLY[: 7 - EARLY_SIDE] + AFTER_ONLY[EARLY_SIDE:]
INNER_TO_BEFORE, INNER_TO_AFTER = slice(0, 6 + EARLY_SIDE), slice(EARLY_SIDE, 6 + 2 * EARLY_SIDE)
OUTER_TO_BEFORE, OUTER_TO_AFTER = slice(0, 7 - EARLY_SIDE), slice(7 - EARLY_SIDE, 14 - 2 * EARLY_SIDE)


def ranks(row, col, depth):
    core, z_half = row & 1, (row >> 1) & 1
    col_rank = col ^ (3 * (core ^ z_half))
    return col_rank, depth ^ (3 * (col_rank & 1))


def place():
    return tuple(lax.axis_index(axis) for axis in EVERY)


def pack_kernel(last_row, density, mask, *outs):
    row, col, depth = place()
    col_rank, depth_rank = ranks(row, col, depth)

    def weight(rank, block_row, slot):
        value = mask[slot, rank * OWN + block_row].astype(jnp.float32)
        if block_row + slot < 2:
            value = jnp.where((row == 0) & (rank == 0), 0.0, value)
        if block_row + slot > OWN + 1:
            value = jnp.where((row == last_row) & (rank == 15), 0.0, value)
        return value

    for k in range(4):
        for other in range(4):
            rank = (col_rank ^ k) * 4 + other
            for index, (block_row, slot) in enumerate(INNER):
                outs[k][0, other, index] = density[rank * OWN + block_row, slot] * weight(rank, block_row, slot)
            rank = other * 4 + (depth ^ (3 * (other & 1)) ^ k)
            for index, (block_row, slot) in enumerate(OUTER):
                outs[4 + k][other, 0, index] = density[rank * OWN + block_row, slot] * weight(rank, block_row, slot)


def pack(density, mask):
    vmem = pl.BlockSpec(memory_space=pltpu.VMEM)
    smem = pl.BlockSpec(memory_space=pltpu.SMEM)
    inner = jax.ShapeDtypeStruct((1, 4, len(INNER), 8, BLK), jnp.float32)
    outer = jax.ShapeDtypeStruct((4, 1, len(OUTER), 8, BLK), jnp.float32)
    outs = pl.pallas_call(
        functools.partial(pack_kernel, lax.axis_size("row") - 1),
        out_shape=[inner] * 4 + [outer] * 4,
        in_specs=[vmem, smem],
        out_specs=[vmem] * 8,
        compiler_params=pltpu.CompilerParams(vmem_limit_bytes=16 * 1024 * 1024),
        cost_estimate=pl.CostEstimate(flops=10**6, bytes_accessed=4 * 1024 * 1024, transcendentals=0),
    )(density, mask)
    return list(outs[:4]), list(outs[4:])


EARLY_AFTER = [(row + OWN, slot) for row, slot in INNER[INNER_TO_BEFORE]]
EARLY_BEFORE = [(row - OWN, slot) for row, slot in INNER[INNER_TO_AFTER]]
LATE_AFTER = [(row + OWN, slot) for row, slot in OUTER[OUTER_TO_BEFORE]]
LATE_BEFORE = [(row - OWN, slot) for row, slot in OUTER[OUTER_TO_AFTER]]
TILES = [(0, 1), (5, 4)] + [(pair, column) for pair in range(1, 5) for column in range(pair - 1, pair + 2)]
MINE = (2, 3)


def at(row, slot):
    return row + 4, row + slot + 2


def split_block(value):
    rounded = value.astype(jnp.bfloat16)
    return rounded, (value - rounded.astype(jnp.float32)).astype(jnp.bfloat16)


def put_block(row, column, parts, high, low):
    rows, columns = slice(row * BLK, (row + 1) * BLK), slice(column * BLK, (column + 1) * BLK)
    high[rows, columns], low[rows, columns] = parts


def product(left_high, left_low, right_high, right_low):
    def dot(a, b):
        return jnp.dot(a, b, preferred_element_type=jnp.float32)

    return dot(left_high, right_high) + (dot(left_high, right_low) + dot(left_low, right_high))


def tile(first, end):
    return slice(first * PAIR, end * PAIR)


def early_kernel(outer, inner, inner_after, inner_before, high, low, square):
    there = set()
    for source, blocks in ((outer, OUTER), (inner, INNER), (inner_after, EARLY_AFTER), (inner_before, EARLY_BEFORE)):
        for index, block in enumerate(blocks):
            put_block(*at(*block), split_block(source[:, index].reshape(BLK, BLK)), high, low)
            there.add(at(*block))
    zero = jnp.zeros((BLK, BLK), jnp.bfloat16)
    for pair, outside in TILES:
        for row in (2 * pair, 2 * pair + 1):
            for column in (2 * outside, 2 * outside + 1):
                if (row, column) not in there:
                    put_block(row, column, (zero, zero), high, low)
    for pair in MINE:
        mine = tile(pair, pair + 1)
        for column in range(pair - 2, pair + 3):
            inside, outside = tile(max(pair, column) - 1, min(pair, column) + 2), tile(column, column + 1)
            square[pair - MINE[0], :, tile(column - pair + 2, column - pair + 3)] = product(
                high[mine, inside], low[mine, inside], high[inside, outside], low[inside, outside]
            )


def early_part(*operands):
    vmem = pl.BlockSpec(memory_space=pltpu.VMEM)
    window = 12 * BLK
    part = jax.ShapeDtypeStruct((window, window), jnp.bfloat16)
    return pl.pallas_call(
        early_kernel,
        out_shape=(part, part, jax.ShapeDtypeStruct((2, PAIR, 5 * PAIR), jnp.float32)),
        in_specs=[vmem] * 4,
        out_specs=(vmem, vmem, vmem),
        compiler_params=pltpu.CompilerParams(vmem_limit_bytes=24 * 1024 * 1024),
        cost_estimate=pl.CostEstimate(flops=2 * 3 * 18 * PAIR**3, bytes_accessed=16 * 1024 * 1024, transcendentals=0),
    )(*operands)


def late_kernel(after, before, high_in, low_in, square, square_mask, out_mask, *refs):
    *outs, high, low, late_high, late_low, square_high, square_low = refs
    col_rank, depth_rank = ranks(*place())
    first = (col_rank * 4 + depth_rank) * OWN
    late = {}
    for side, (source, blocks) in enumerate(((before, LATE_BEFORE), (after, LATE_AFTER))):
        there = set()
        pair = 1 + 3 * side
        for index, block in enumerate(blocks):
            row, column = at(*block)
            parts = split_block(source[:, index].reshape(BLK, BLK))
            put_block(row, column, parts, high, low)
            put_block(2 * side + row - 2 * pair, column - 2 * pair + 2, parts, late_high, late_low)
            there.add((row, column))
        zero = jnp.zeros((BLK, BLK), jnp.bfloat16)
        late[pair + 1 - 2 * side] = (pair, side, {column // 2 for _, column in there})
        for row in (2 * pair, 2 * pair + 1):
            for column in range(2 * pair - 2, 2 * pair + 4):
                if (row, column) not in there:
                    put_block(2 * side + row - 2 * pair, column - 2 * pair + 2, (zero, zero), late_high, late_low)
    for pair in MINE:
        mine = tile(pair, pair + 1)
        kept = {}
        source, side, touched = late[pair]
        for column in range(pair - 2, pair + 3):
            value = square[pair - MINE[0], :, tile(column - pair + 2, column - pair + 3)]
            if column in touched:
                inside, rows, outside = tile(source, source + 1), tile(side, side + 1), tile(column - source + 1, column - source + 2)
                value += product(high[mine, inside], low[mine, inside], late_high[rows, outside], late_low[rows, outside])
            for half in range(2):
                for part in range(2):
                    slot = 2 * (column - pair) + part - half + 4
                    block = value[half * BLK : (half + 1) * BLK, part * BLK : (part + 1) * BLK]
                    row = 2 * (pair - MINE[0]) + half
                    if 0 <= slot < 9:
                        block = block * square_mask[slot, first + row].astype(jnp.float32)
                    if 2 <= slot < 7:
                        kept[half, slot - 2] = block
                    put_block(half, 2 * column + part, split_block(block), square_high, square_low)
        for column in range(pair - 1, pair + 2):
            inside, outside = tile(column - 1, column + 2), tile(column, column + 1)
            cube = product(square_high[:, inside], square_low[:, inside], high[inside, outside], low[inside, outside])
            for half in range(2):
                for part in range(2):
                    slot = 2 * (column - pair) + part - half + 2
                    row = 2 * (pair - MINE[0]) + half
                    if 0 <= slot < 5:
                        block = cube[half * BLK : (half + 1) * BLK, part * BLK : (part + 1) * BLK]
                        gate = out_mask[slot, first + row].astype(jnp.float32)
                        value = (gate * (3.0 * kept[half, slot] - 2.0 * block)).reshape(16, 8, BLK)
                        index = row * 5 + slot
                        if index < FIRST_OUT:
                            outs[0][:, index] = value
                        else:
                            outs[1][:, index - FIRST_OUT] = value


def late_part(*operands):
    vmem = pl.BlockSpec(memory_space=pltpu.VMEM)
    smem = pl.BlockSpec(memory_space=pltpu.SMEM)
    window = 12 * BLK
    part = jax.ShapeDtypeStruct((window, window), jnp.bfloat16)
    return pl.pallas_call(
        late_kernel,
        out_shape=[jax.ShapeDtypeStruct((16, count, 8, BLK), jnp.float32) for count in (FIRST_OUT, 20 - FIRST_OUT)] + [part] * 2,
        in_specs=[vmem] * 5 + [smem] * 2,
        out_specs=[vmem] * 4,
        scratch_shapes=[pltpu.VMEM((2 * PAIR, 3 * PAIR), jnp.bfloat16)] * 2 + [pltpu.VMEM((PAIR, window), jnp.bfloat16)] * 2,
        input_output_aliases={2: 2, 3: 3},
        compiler_params=pltpu.CompilerParams(vmem_limit_bytes=24 * 1024 * 1024),
        cost_estimate=pl.CostEstimate(flops=2 * 3 * 22 * PAIR**3, bytes_accessed=4 * 1024 * 1024, transcendentals=0),
    )(*operands)[:2]


def send(pieces, axis):
    size = lax.axis_size(axis)
    return pieces[:1] + [lax.ppermute(pieces[k], axis, [(i, i ^ k) for i in range(size)]) for k in range(1, size)]


def cut(value, dim, far):
    return [lax.dynamic_slice_in_dim(value, far ^ k, 1, dim) for k in range(value.shape[dim])]


def join(pieces, dim, near, early_first=True):
    stack = jnp.concatenate(pieces[::-1] if early_first else pieces, axis=dim)
    last = (len(pieces) - 1) * early_first
    return jnp.concatenate([lax.dynamic_slice_in_dim(stack, near ^ j ^ last, 1, dim) for j in range(len(pieces))], axis=dim)


def swap(value, axis, dim, near, far):
    return join(send(cut(value, dim, far), axis), dim, near)


def gather_kernel(by_col, before_part, after_part, *refs):
    pieces, (whole, to_before, to_after) = refs[:4], refs[4:]
    row, col, depth = place()
    for k, piece in enumerate(pieces):
        for other in range(4):
            if by_col:
                value, layer = piece[0, other], (col ^ k) * 4 + other
            else:
                value, layer = piece[other, 0], other * 4 + (depth ^ k)
            whole[layer] = value
            to_before[layer] = value[before_part]
            to_after[layer] = value[after_part]


def gather(pieces, by_col, before_part, after_part):
    vmem = pl.BlockSpec(memory_space=pltpu.VMEM)
    count = pieces[0].shape[2]
    counts = (count, before_part.stop - before_part.start, after_part.stop - after_part.start)
    return pl.pallas_call(
        functools.partial(gather_kernel, by_col, before_part, after_part),
        out_shape=[jax.ShapeDtypeStruct((16, n, 8, BLK), jnp.float32) for n in counts],
        in_specs=[vmem] * 4,
        out_specs=[vmem] * 3,
        compiler_params=pltpu.CompilerParams(vmem_limit_bytes=16 * 1024 * 1024),
        cost_estimate=pl.CostEstimate(flops=0, bytes_accessed=0, transcendentals=0),
    )(*pieces)


def chain(rows):
    places = [(row, col, depth) for row in range(rows) for col in range(4) for depth in range(4)]
    places.sort(key=lambda at: (at[0], *ranks(*at)))
    return [row * 16 + col * 4 + depth for row, col, depth in places]


def on_device(density, mask_band, mask_square, mask_out):
    row, col, depth = place()
    col_rank, depth_rank = ranks(row, col, depth)
    order = chain(lax.axis_size("row"))
    up = list(zip(order[:-1], order[1:]))
    down = list(zip(order[1:], order[:-1]))

    def halo(to_before, to_after):
        after = lax.ppermute(to_before, EVERY, down)
        before = lax.ppermute(to_after, EVERY, up)
        return after, before

    inner, outer = pack(density, mask_band.T)
    inner = join(send(inner, "col"), 0, col)
    outer = join(send(outer, "depth"), 1, depth)
    outer = swap(outer, "col", 0, col, col_rank).reshape(16, len(OUTER), 8, BLK)
    inner = send(cut(inner, 1, depth_rank), "depth")
    inner, *inner_halo = gather(inner, False, INNER_TO_BEFORE, INNER_TO_AFTER)
    outer_halo = outer[:, OUTER_TO_BEFORE], outer[:, OUTER_TO_AFTER]
    early = early_part(outer, inner, *halo(*inner_halo))
    late = halo(*outer_halo)
    lower, upper = late_part(*late, *early, mask_square.T, mask_out.T)
    lower = lower.reshape(4, 4, FIRST_OUT, 8, BLK)
    upper = upper.reshape(4, 4, 20 - FIRST_OUT, 8, BLK)
    lower = join(send(cut(lower, 0, col), "col"), 0, col_rank, False)
    upper = swap(upper, "depth", 1, depth_rank, depth)
    upper = send(cut(upper, 0, col), "col")
    upper[1], lower = lax.optimization_barrier((upper[1], lower))
    upper = join(upper, 0, col_rank)
    lower = send(cut(lower, 1, depth), "depth")
    turns = [join([piece[turn::2] for piece in lower], 1, depth ^ (3 * turn)) for turn in range(2)]
    lower = jnp.stack(turns, axis=1).reshape(4, 4, FIRST_OUT, 8, BLK)
    return jnp.concatenate([lower, upper], axis=2).reshape(density.shape)


def solution(mesh):
    return jax.shard_map(
        on_device,
        mesh=mesh,
        in_specs=(
            P("row", None, ("col", "depth"), None),
            P("row", None),
            P("row", None),
            P("row", None),
        ),
        out_specs=P("row", None, ("col", "depth"), None),
        check_vma=False,
    )
```

```python
import functools

import jax
import jax.numpy as jnp
from jax import lax
from jax.experimental import pallas as pl
from jax.experimental.pallas import tpu as pltpu
from jax.sharding import PartitionSpec as P

BLK = 128
OWN = 4
HALO = 4
PAIR = 2 * BLK
FIRST_OUT = 9
EVERY = ("row", "col", "depth")

BEFORE_ONLY = [(0, s) for s in range(4)] + [(1, s) for s in range(3)]
BOTH = [(0, 4), (1, 3), (1, 4), (2, 0), (2, 1), (3, 0)]
AFTER_ONLY = [(2, s) for s in range(2, 5)] + [(3, s) for s in range(1, 5)]
EARLY_SIDE = 2
INNER = BEFORE_ONLY[7 - EARLY_SIDE :] + BOTH + AFTER_ONLY[:EARLY_SIDE]
OUTER = BEFORE_ONLY[: 7 - EARLY_SIDE] + AFTER_ONLY[EARLY_SIDE:]
INNER_TO_BEFORE, INNER_TO_AFTER = slice(0, 6 + EARLY_SIDE), slice(EARLY_SIDE, 6 + 2 * EARLY_SIDE)
OUTER_TO_BEFORE, OUTER_TO_AFTER = slice(0, 7 - EARLY_SIDE), slice(7 - EARLY_SIDE, 14 - 2 * EARLY_SIDE)


def ranks(row, col, depth):
    core, z_half = row & 1, (row >> 1) & 1
    col_rank = col ^ (3 * (core ^ z_half))
    return col_rank, depth ^ (3 * (col_rank & 1))


def place():
    return tuple(lax.axis_index(axis) for axis in EVERY)


def pack_kernel(last_row, density, mask, *outs):
    row, col, depth = place()
    col_rank, depth_rank = ranks(row, col, depth)

    def weight(rank, block_row, slot):
        value = mask[slot, rank * OWN + block_row].astype(jnp.float32)
        if block_row + slot < 2:
            value = jnp.where((row == 0) & (rank == 0), 0.0, value)
        if block_row + slot > OWN + 1:
            value = jnp.where((row == last_row) & (rank == 15), 0.0, value)
        return value

    for k in range(4):
        for other in range(4):
            rank = (col_rank ^ k) * 4 + other
            for index, (block_row, slot) in enumerate(INNER):
                outs[k][0, other, index] = density[rank * OWN + block_row, slot] * weight(rank, block_row, slot)
            rank = other * 4 + (depth ^ (3 * (other & 1)) ^ k)
            for index, (block_row, slot) in enumerate(OUTER):
                outs[4 + k][other, 0, index] = density[rank * OWN + block_row, slot] * weight(rank, block_row, slot)


def pack(density, mask):
    vmem = pl.BlockSpec(memory_space=pltpu.VMEM)
    smem = pl.BlockSpec(memory_space=pltpu.SMEM)
    inner = jax.ShapeDtypeStruct((1, 4, len(INNER), 8, BLK), jnp.float32)
    outer = jax.ShapeDtypeStruct((4, 1, len(OUTER), 8, BLK), jnp.float32)
    outs = pl.pallas_call(
        functools.partial(pack_kernel, lax.axis_size("row") - 1),
        out_shape=[inner] * 4 + [outer] * 4,
        in_specs=[vmem, smem],
        out_specs=[vmem] * 8,
        compiler_params=pltpu.CompilerParams(vmem_limit_bytes=16 * 1024 * 1024),
        cost_estimate=pl.CostEstimate(flops=10**6, bytes_accessed=4 * 1024 * 1024, transcendentals=0),
    )(density, mask)
    return list(outs[:4]), list(outs[4:])


EARLY_AFTER = [(row + OWN, slot) for row, slot in INNER[INNER_TO_BEFORE]]
EARLY_BEFORE = [(row - OWN, slot) for row, slot in INNER[INNER_TO_AFTER]]
LATE_AFTER = [(row + OWN, slot) for row, slot in OUTER[OUTER_TO_BEFORE]]
LATE_BEFORE = [(row - OWN, slot) for row, slot in OUTER[OUTER_TO_AFTER]]
TILES = [(0, 1), (5, 4)] + [(pair, column) for pair in range(1, 5) for column in range(pair - 1, pair + 2)]
MINE = (2, 3)


def at(row, slot):
    return row + 4, row + slot + 2


def split_block(value):
    rounded = value.astype(jnp.bfloat16)
    return rounded, (value - rounded.astype(jnp.float32)).astype(jnp.bfloat16)


def put_block(row, column, parts, high, low):
    rows, columns = slice(row * BLK, (row + 1) * BLK), slice(column * BLK, (column + 1) * BLK)
    high[rows, columns], low[rows, columns] = parts


def product(left_high, left_low, right_high, right_low):
    def dot(a, b):
        return jnp.dot(a, b, preferred_element_type=jnp.float32)

    return dot(left_high, right_high) + (dot(left_high, right_low) + dot(left_low, right_high))


def tile(first, end):
    return slice(first * PAIR, end * PAIR)


def early_kernel(outer, inner, inner_after, inner_before, high, low, square):
    there = set()
    for source, blocks in ((outer, OUTER), (inner, INNER), (inner_after, EARLY_AFTER), (inner_before, EARLY_BEFORE)):
        for index, block in enumerate(blocks):
            put_block(*at(*block), split_block(source[:, index].reshape(BLK, BLK)), high, low)
            there.add(at(*block))
    zero = jnp.zeros((BLK, BLK), jnp.bfloat16)
    for pair, outside in TILES:
        for row in (2 * pair, 2 * pair + 1):
            for column in (2 * outside, 2 * outside + 1):
                if (row, column) not in there:
                    put_block(row, column, (zero, zero), high, low)
    for pair in MINE:
        mine = tile(pair, pair + 1)
        for column in range(pair - 2, pair + 3):
            inside, outside = tile(max(pair, column) - 1, min(pair, column) + 2), tile(column, column + 1)
            square[pair - MINE[0], :, tile(column - pair + 2, column - pair + 3)] = product(
                high[mine, inside], low[mine, inside], high[inside, outside], low[inside, outside]
            )


def early_part(*operands):
    vmem = pl.BlockSpec(memory_space=pltpu.VMEM)
    window = 12 * BLK
    part = jax.ShapeDtypeStruct((window, window), jnp.bfloat16)
    return pl.pallas_call(
        early_kernel,
        out_shape=(part, part, jax.ShapeDtypeStruct((2, PAIR, 5 * PAIR), jnp.float32)),
        in_specs=[vmem] * 4,
        out_specs=(vmem, vmem, vmem),
        compiler_params=pltpu.CompilerParams(vmem_limit_bytes=24 * 1024 * 1024),
        cost_estimate=pl.CostEstimate(flops=2 * 3 * 18 * PAIR**3, bytes_accessed=16 * 1024 * 1024, transcendentals=0),
    )(*operands)


def late_kernel(after, before, high_in, low_in, square, square_mask, out_mask, *refs):
    *outs, high, low, late_high, late_low, square_high, square_low = refs
    col_rank, depth_rank = ranks(*place())
    first = (col_rank * 4 + depth_rank) * OWN
    late = {}
    for side, (source, blocks) in enumerate(((before, LATE_BEFORE), (after, LATE_AFTER))):
        there = set()
        pair = 1 + 3 * side
        for index, block in enumerate(blocks):
            row, column = at(*block)
            parts = split_block(source[:, index].reshape(BLK, BLK))
            put_block(row, column, parts, high, low)
            put_block(2 * side + row - 2 * pair, column - 2 * pair + 2, parts, late_high, late_low)
            there.add((row, column))
        zero = jnp.zeros((BLK, BLK), jnp.bfloat16)
        late[pair + 1 - 2 * side] = (pair, side, {column // 2 for _, column in there})
        for row in (2 * pair, 2 * pair + 1):
            for column in range(2 * pair - 2, 2 * pair + 4):
                if (row, column) not in there:
                    put_block(2 * side + row - 2 * pair, column - 2 * pair + 2, (zero, zero), late_high, late_low)
    for pair in MINE:
        mine = tile(pair, pair + 1)
        kept = {}
        source, side, touched = late[pair]
        for column in range(pair - 2, pair + 3):
            value = square[pair - MINE[0], :, tile(column - pair + 2, column - pair + 3)]
            if column in touched:
                inside, rows, outside = tile(source, source + 1), tile(side, side + 1), tile(column - source + 1, column - source + 2)
                value += product(high[mine, inside], low[mine, inside], late_high[rows, outside], late_low[rows, outside])
            for half in range(2):
                for part in range(2):
                    slot = 2 * (column - pair) + part - half + 4
                    block = value[half * BLK : (half + 1) * BLK, part * BLK : (part + 1) * BLK]
                    row = 2 * (pair - MINE[0]) + half
                    if 0 <= slot < 9:
                        block = block * square_mask[slot, first + row].astype(jnp.float32)
                    if 2 <= slot < 7:
                        kept[half, slot - 2] = block
                    put_block(half, 2 * column + part, split_block(block), square_high, square_low)
        for column in range(pair - 1, pair + 2):
            inside, outside = tile(column - 1, column + 2), tile(column, column + 1)
            cube = product(square_high[:, inside], square_low[:, inside], high[inside, outside], low[inside, outside])
            for half in range(2):
                for part in range(2):
                    slot = 2 * (column - pair) + part - half + 2
                    row = 2 * (pair - MINE[0]) + half
                    if 0 <= slot < 5:
                        block = cube[half * BLK : (half + 1) * BLK, part * BLK : (part + 1) * BLK]
                        gate = out_mask[slot, first + row].astype(jnp.float32)
                        value = (gate * (3.0 * kept[half, slot] - 2.0 * block)).reshape(16, 8, BLK)
                        index = row * 5 + slot
                        if index < FIRST_OUT:
                            outs[0][:, index] = value
                        else:
                            outs[1][:, index - FIRST_OUT] = value


def late_part(*operands):
    vmem = pl.BlockSpec(memory_space=pltpu.VMEM)
    smem = pl.BlockSpec(memory_space=pltpu.SMEM)
    window = 12 * BLK
    part = jax.ShapeDtypeStruct((window, window), jnp.bfloat16)
    return pl.pallas_call(
        late_kernel,
        out_shape=[jax.ShapeDtypeStruct((16, count, 8, BLK), jnp.float32) for count in (FIRST_OUT, 20 - FIRST_OUT)] + [part] * 2,
        in_specs=[vmem] * 5 + [smem] * 2,
        out_specs=[vmem] * 4,
        scratch_shapes=[pltpu.VMEM((2 * PAIR, 3 * PAIR), jnp.bfloat16)] * 2 + [pltpu.VMEM((PAIR, window), jnp.bfloat16)] * 2,
        input_output_aliases={2: 2, 3: 3},
        compiler_params=pltpu.CompilerParams(vmem_limit_bytes=24 * 1024 * 1024),
        cost_estimate=pl.CostEstimate(flops=2 * 3 * 22 * PAIR**3, bytes_accessed=4 * 1024 * 1024, transcendentals=0),
    )(*operands)[:2]


def send(pieces, axis):
    size = lax.axis_size(axis)
    return pieces[:1] + [lax.ppermute(pieces[k], axis, [(i, i ^ k) for i in range(size)]) for k in range(1, size)]


def cut(value, dim, far):
    return [lax.dynamic_slice_in_dim(value, far ^ k, 1, dim) for k in range(value.shape[dim])]


def join(pieces, dim, near, early_first=True):
    stack = jnp.concatenate(pieces[::-1] if early_first else pieces, axis=dim)
    last = (len(pieces) - 1) * early_first
    return jnp.concatenate([lax.dynamic_slice_in_dim(stack, near ^ j ^ last, 1, dim) for j in range(len(pieces))], axis=dim)


def swap(value, axis, dim, near, far):
    return join(send(cut(value, dim, far), axis), dim, near)


def gather_kernel(by_col, before_part, after_part, *refs):
    pieces, (whole, to_before, to_after) = refs[:4], refs[4:]
    row, col, depth = place()
    for k, piece in enumerate(pieces):
        for other in range(4):
            if by_col:
                value, layer = piece[0, other], (col ^ k) * 4 + other
            else:
                value, layer = piece[other, 0], other * 4 + (depth ^ k)
            whole[layer] = value
            to_before[layer] = value[before_part]
            to_after[layer] = value[after_part]


def gather(pieces, by_col, before_part, after_part):
    vmem = pl.BlockSpec(memory_space=pltpu.VMEM)
    count = pieces[0].shape[2]
    counts = (count, before_part.stop - before_part.start, after_part.stop - after_part.start)
    return pl.pallas_call(
        functools.partial(gather_kernel, by_col, before_part, after_part),
        out_shape=[jax.ShapeDtypeStruct((16, n, 8, BLK), jnp.float32) for n in counts],
        in_specs=[vmem] * 4,
        out_specs=[vmem] * 3,
        compiler_params=pltpu.CompilerParams(vmem_limit_bytes=16 * 1024 * 1024),
        cost_estimate=pl.CostEstimate(flops=0, bytes_accessed=0, transcendentals=0),
    )(*pieces)


def chain(rows):
    places = [(row, col, depth) for row in range(rows) for col in range(4) for depth in range(4)]
    places.sort(key=lambda at: (at[0], *ranks(*at)))
    return [row * 16 + col * 4 + depth for row, col, depth in places]


def on_device(density, mask_band, mask_square, mask_out):
    row, col, depth = place()
    col_rank, depth_rank = ranks(row, col, depth)
    order = chain(lax.axis_size("row"))
    up = list(zip(order[:-1], order[1:]))
    down = list(zip(order[1:], order[:-1]))

    def halo(to_before, to_after):
        after = lax.ppermute(to_before, EVERY, down)
        before = lax.ppermute(to_after, EVERY, up)
        return after, before

    inner, outer = pack(density, mask_band.T)
    inner = join(send(inner, "col"), 0, col)
    outer = join(send(outer, "depth"), 1, depth)
    outer = swap(outer, "col", 0, col, col_rank).reshape(16, len(OUTER), 8, BLK)
    inner = send(cut(inner, 1, depth_rank), "depth")
    inner, *inner_halo = gather(inner, False, INNER_TO_BEFORE, INNER_TO_AFTER)
    outer_halo = outer[:, OUTER_TO_BEFORE], outer[:, OUTER_TO_AFTER]
    early = early_part(outer, inner, *halo(*inner_halo))
    late = halo(*outer_halo)
    lower, upper = late_part(*late, *early, mask_square.T, mask_out.T)
    lower = lower.reshape(4, 4, FIRST_OUT, 8, BLK)
    upper = upper.reshape(4, 4, 20 - FIRST_OUT, 8, BLK)
    lower = join(send(cut(lower, 0, col), "col"), 0, col_rank, False)
    upper = swap(upper, "depth", 1, depth_rank, depth)
    upper = send(cut(upper, 0, col), "col")
    upper[1], lower = lax.optimization_barrier((upper[1], lower))
    upper = join(upper, 0, col_rank)
    lower = send(cut(lower, 1, depth), "depth")
    turns = [join([piece[turn::2] for piece in lower], 1, depth ^ (3 * turn)) for turn in range(2)]
    lower = jnp.stack(turns, axis=1).reshape(4, 4, FIRST_OUT, 8, BLK)
    return jnp.concatenate([lower, upper], axis=2).reshape(density.shape)


def solution(mesh):
    return jax.shard_map(
        on_device,
        mesh=mesh,
        in_specs=(
            P("row", None, ("col", "depth"), None),
            P("row", None),
            P("row", None),
            P("row", None),
        ),
        out_specs=P("row", None, ("col", "depth"), None),
        check_vma=False,
    )
```
